768 devices in a mesh: seq: 16 (over z_lo, x), res: 48 (over z_hi, y, core).
Axes of the slice: x: 4, y: 8, z: 12 (z_hi: 3, z_lo: 4; z = z_hi * 4 + z_lo), core: 2. Of those that a mesh axis runs over, the one named last changes fastest.
Arguments:
- alignment_tensor: float32 [768, 768, 256], P('seq', 'res'), may hold values from -24 to 24
- standardizer_factors: float32 [3, 256], replicated, may hold values from 0.25 to 1.75
- standardizer_offsets: float32 [3, 256], replicated, may hold values from -3 to 3
- horizontal_entry_matrix: bfloat16 [256, 1024], replicated, may hold values from -4 to 4
- horizontal_sigmoid_offset: float32 [256], replicated, may hold values from -4 to 4
- horizontal_exit_matrix: bfloat16 [256, 256], replicated, may hold values from -1 to 1
- horizontal_exit_offset: float32 [256], replicated, may hold values from -2 to 2
- vertical_entry_matrix: bfloat16 [256, 1024], replicated, may hold values from -4 to 4
- vertical_sigmoid_offset: float32 [256], replicated, may hold values from -4 to 4
- vertical_exit_matrix: bfloat16 [256, 256], replicated, may hold values from -1 to 1
- vertical_exit_offset: float32 [256], replicated, may hold values from -2 to 2
- feedforward_first_matrix: bfloat16 [256, 1024], replicated, may hold values from -0.375 to 0.375
- feedforward_first_offset: float32 [1024], replicated, may hold values from -3 to 3
- feedforward_second_matrix: bfloat16 [1024, 256], replicated, may hold values from -0.25 to 0.25
- feedforward_second_offset: float32 [256], replicated, may hold values from -2 to 2
Outputs:
- updated_msa: float32 [768, 768, 256], P('seq', 'res')
The draws below stay inside these ranges and needn't reach their ends.
All inputs are finite; a program needn't handle non-finite values.
Results may differ from the reference program's by a relative error of at most 0.012.
Values may be sent and summed in bfloat16 or wider, within the bound.
No kernel may reach another device: no remote copies, remote signals or barrier semaphores. Data moves between devices by JAX's collectives and lax.ppermute only.
A program may use at most 32 MiB of HBM per device.

```python
import jax
import jax.numpy as jnp
from jax import lax

C = 256
HEADS = 8
FF = 1024
SEQS = 768
RESIDUES = 768


def draw_alignment_tensor(key, part):
    own_key = jax.random.fold_in(key, 13)
    base = jax.random.normal(jax.random.fold_in(own_key, 1), (SEQS, RESIDUES, C), jnp.float32)
    return jnp.clip(base, -24.0, 24.0)


def projection_draw(key, salt):
    own_key = jax.random.fold_in(key, salt)
    columns = jnp.arange(4 * C)
    column_scale = jnp.where(columns < 2 * C, 1.4, 1.0)
    base = jax.random.normal(own_key, (C, 4 * C), jnp.float32) * column_scale / jnp.sqrt(jnp.float32(C))
    return jnp.clip(base, -4.0, 4.0)


def draw_horizontal_entry_matrix(key, part):
    return projection_draw(key, 21).astype(jnp.bfloat16)


def draw_vertical_entry_matrix(key, part):
    return projection_draw(key, 22).astype(jnp.bfloat16)


def gaussian(key, dims, scale, most, dtype=jnp.bfloat16):
    values = jax.random.normal(key, dims, jnp.float32) * scale
    return jnp.minimum(jnp.maximum(values, -most), most).astype(dtype)


def setup_inputs(seed: int = 0) -> dict:
    keys = jax.random.split(jax.random.key(seed), 16)
    alignment_tensor = draw_alignment_tensor(jax.random.fold_in(keys[15], 71), 0)
    standardizer_factors = jnp.clip(1.0 + 0.15 * jax.random.normal(keys[1], (3, C), jnp.float32), 0.25, 1.75)
    standardizer_offsets = gaussian(keys[2], (3, C), 0.5, 3.0, jnp.float32)
    horizontal_entry_matrix = draw_horizontal_entry_matrix(jax.random.fold_in(keys[15], 71), 0)
    horizontal_sigmoid_offset = gaussian(keys[4], (C,), 1.0, 4.0, jnp.float32)
    horizontal_exit_matrix = gaussian(keys[5], (C, C), (C // 8) ** -0.5, 1.0)
    horizontal_exit_offset = gaussian(keys[6], (C,), 0.3, 2.0, jnp.float32)
    vertical_entry_matrix = draw_vertical_entry_matrix(jax.random.fold_in(keys[15], 71), 0)
    vertical_sigmoid_offset = gaussian(keys[8], (C,), 1.0, 4.0, jnp.float32)
    vertical_exit_matrix = gaussian(keys[9], (C, C), (C // 8) ** -0.5, 1.0)
    vertical_exit_offset = gaussian(keys[10], (C,), 0.3, 2.0, jnp.float32)
    feedforward_first_matrix = gaussian(keys[11], (C, FF), C ** -0.5, 0.375)
    feedforward_first_offset = gaussian(keys[12], (FF,), 0.5, 3.0, jnp.float32)
    feedforward_second_matrix = gaussian(keys[13], (FF, C), (FF // 2) ** -0.5, 0.25)
    feedforward_second_offset = gaussian(keys[14], (C,), 0.3, 2.0, jnp.float32)
    return {"alignment_tensor": alignment_tensor, "standardizer_factors": standardizer_factors, "standardizer_offsets": standardizer_offsets, "horizontal_entry_matrix": horizontal_entry_matrix, "horizontal_sigmoid_offset": horizontal_sigmoid_offset, "horizontal_exit_matrix": horizontal_exit_matrix, "horizontal_exit_offset": horizontal_exit_offset, "vertical_entry_matrix": vertical_entry_matrix, "vertical_sigmoid_offset": vertical_sigmoid_offset, "vertical_exit_matrix": vertical_exit_matrix, "vertical_exit_offset": vertical_exit_offset, "feedforward_first_matrix": feedforward_first_matrix, "feedforward_first_offset": feedforward_first_offset, "feedforward_second_matrix": feedforward_second_matrix, "feedforward_second_offset": feedforward_second_offset}


def standardize_features(values, gain, shift):
    row_mean = lax.optimization_barrier(jnp.mean(values, axis=-1, keepdims=True))
    centred = values - row_mean
    variance = lax.optimization_barrier(jnp.mean(centred * centred, axis=-1, keepdims=True))
    return (centred * lax.rsqrt(variance + 1e-05) * gain + shift).astype(jnp.bfloat16)

def final_mapping(source, weight, offset):
    dims_in = source.shape
    flat = jnp.dot(source.reshape(-1, dims_in[-1]), weight, preferred_element_type=jnp.float32) + offset
    return flat.reshape(dims_in[:-1] + (weight.shape[1],))

def attention_single(normed, proj, gate_bias):
    length, channels = normed.shape
    head_size = channels // HEADS
    projected = jnp.dot(normed, proj, preferred_element_type=jnp.float32)
    query = (projected[:, :channels] * head_size ** (-0.5)).astype(jnp.bfloat16)
    key_rows = projected[:, channels:2 * channels].astype(jnp.bfloat16)
    value_rows = projected[:, 2 * channels:3 * channels].astype(jnp.bfloat16)
    gate_value = jax.nn.sigmoid(projected[:, 3 * channels:] + gate_bias)
    query_f = query.astype(jnp.float32).reshape(length, HEADS, head_size)
    key_f = key_rows.astype(jnp.float32).reshape(length, HEADS, head_size)
    value_f = value_rows.astype(jnp.float32).reshape(length, HEADS, head_size)
    scores = jnp.einsum('qhd,khd->hqk', query_f, key_f, precision=lax.Precision.HIGHEST)
    peak_score = lax.optimization_barrier(jnp.max(scores, axis=-1, keepdims=True))
    weights = jnp.exp(scores - peak_score)
    row_total = lax.optimization_barrier(jnp.sum(weights, axis=-1, keepdims=True))
    probabilities = (weights / row_total).astype(jnp.bfloat16).astype(jnp.float32)
    mixed = jnp.einsum('hqk,khd->qhd', probabilities, value_f, precision=lax.Precision.HIGHEST)
    return (gate_value * mixed.reshape(length, channels)).astype(jnp.bfloat16)

def reference(alignment_tensor, standardizer_factors, standardizer_offsets, horizontal_entry_matrix, horizontal_sigmoid_offset, horizontal_exit_matrix, horizontal_exit_offset, vertical_entry_matrix, vertical_sigmoid_offset, vertical_exit_matrix, vertical_exit_offset, feedforward_first_matrix, feedforward_first_offset, feedforward_second_matrix, feedforward_second_offset):
    standardized_horizontal = standardize_features(alignment_tensor, standardizer_factors[0], standardizer_offsets[0])
    horizontal_sigmoid_masked = lax.map(lambda lone_alignment_entry: attention_single(lone_alignment_entry, horizontal_entry_matrix, horizontal_sigmoid_offset), standardized_horizontal)
    alignment_horizontal_done = alignment_tensor + lax.map(lambda lone_alignment_entry: final_mapping(lone_alignment_entry, horizontal_exit_matrix, horizontal_exit_offset), horizontal_sigmoid_masked)
    standardized_vertical = standardize_features(alignment_horizontal_done, standardizer_factors[1], standardizer_offsets[1]).transpose(1, 0, 2)
    vertical_sigmoid_masked = lax.map(lambda lone_alignment_entry: attention_single(lone_alignment_entry, vertical_entry_matrix, vertical_sigmoid_offset), standardized_vertical).transpose(1, 0, 2)
    vertical_done = alignment_horizontal_done + lax.map(lambda lone_alignment_entry: final_mapping(lone_alignment_entry, vertical_exit_matrix, vertical_exit_offset), vertical_sigmoid_masked)

    def transition(lone_alignment_entry):
        normed_trans = standardize_features(lone_alignment_entry, standardizer_factors[2], standardizer_offsets[2])
        inner = jax.nn.relu(final_mapping(normed_trans, feedforward_first_matrix, feedforward_first_offset)).astype(jnp.bfloat16)
        return lone_alignment_entry + final_mapping(inner, feedforward_second_matrix, feedforward_second_offset)
    return lax.map(transition, vertical_done)
```

```python
import functools

import jax
import jax.numpy as jnp
from jax import lax
from jax.experimental import pallas as pl
from jax.experimental.pallas import tpu as pltpu
from jax.sharding import PartitionSpec as P

HEADS = 8
LANES = 128
EPSILON = 1e-05
LOG2E = 1.4426950408889634
VMEM_LIMIT = 48 * 1024 * 1024


def normalize(values, gain, shift):
    row_mean = jnp.mean(values, axis=-1, keepdims=True)
    centred = values - row_mean
    variance = jnp.mean(centred * centred, axis=-1, keepdims=True)
    return (centred * lax.rsqrt(variance + EPSILON) * gain + shift).astype(jnp.bfloat16)


def matmul(left, right):
    return jnp.dot(left, right, preferred_element_type=jnp.float32)


def norm_kernel(values_ref, gain_ref, shift_ref, out_ref):
    out_ref[...] = normalize(values_ref[...], gain_ref[0:1], shift_ref[0:1])


def attention_kernel(normed_ref, entry_ref, gate_ref, out_ref, query_ref, key_ref, value_ref, gated_ref):
    rows, channels = normed_ref.shape
    head_size = channels // HEADS
    per_tile = LANES // head_size
    block = 256
    normed = normed_ref[...]
    query_ref[...] = (
        matmul(normed, entry_ref[:, :channels]) * (LOG2E * head_size**-0.5)
    ).astype(jnp.bfloat16)
    key_ref[...] = matmul(normed, entry_ref[:, channels : 2 * channels]).astype(jnp.bfloat16)
    value_ref[...] = matmul(normed, entry_ref[:, 2 * channels : 3 * channels]).astype(jnp.bfloat16)
    gated_ref[...] = jax.nn.sigmoid(matmul(normed, entry_ref[:, 3 * channels :]) + gate_ref[...])
    lane_head = lax.broadcasted_iota(jnp.int32, (1, LANES), 1) // head_size
    for tile in range(channels // LANES):
        lanes = slice(tile * LANES, (tile + 1) * LANES)
        keys = key_ref[:, lanes]
        values = jnp.concatenate(
            [value_ref[:, lanes], jnp.ones((rows, LANES), jnp.bfloat16)], axis=1
        )
        for start in range(0, rows, block):
            queries = query_ref[start : start + block, lanes]
            mixed = jnp.zeros((block, LANES), jnp.float32)
            for head in range(per_tile):
                mask = (lane_head == head).astype(jnp.float32)
                scores = lax.dot_general(
                    queries * mask.astype(jnp.bfloat16),
                    keys,
                    (((1,), (1,)), ((), ())),
                    preferred_element_type=jnp.float32,
                )
                peak = jnp.max(scores, axis=-1, keepdims=True)
                weights = jnp.exp2(scores - peak).astype(jnp.bfloat16)
                result = matmul(weights, values)
                mixed = jnp.where(lane_head == head, result[:, :LANES] / result[:, LANES:], mixed)
            out_ref[start : start + block, lanes] = (
                gated_ref[start : start + block, lanes] * mixed
            ).astype(jnp.bfloat16)


def turn_kernel(
    residues, base_ref, gated_ref, exit_ref, offset_ref, gain_ref, shift_ref, after_ref, out_ref, after_rows_ref
):
    rows = base_ref.shape[0]
    seqs = rows // residues
    after = base_ref[...] + (matmul(gated_ref[...], exit_ref[...]) + offset_ref[...])
    tiles = range(after_rows_ref.shape[0])
    for tile in tiles:
        after_rows_ref[tile] = after[:, tile * LANES : (tile + 1) * LANES]
    for item in range(residues):
        picked = jnp.concatenate(
            [after_rows_ref.at[tile][pl.ds(item, seqs, stride=residues), :] for tile in tiles], axis=1
        )
        after_ref[item * seqs : (item + 1) * seqs, :] = picked
        out_ref[item * seqs : (item + 1) * seqs, :] = normalize(picked, gain_ref[1:2], shift_ref[1:2])


def transition_kernel(
    residues,
    after_ref,
    gated_ref,
    exit_ref,
    offset_ref,
    gain_ref,
    shift_ref,
    first_ref,
    first_offset_ref,
    second_ref,
    second_offset_ref,
    out_ref,
    final_ref,
):
    rows = after_ref.shape[0]
    seqs = rows // residues
    group = 4
    block = group * seqs
    for start in range(0, rows, block):
        span = slice(start, start + block)
        after = after_ref[span, :] + (matmul(gated_ref[span, :], exit_ref[...]) + offset_ref[...])
        normed = normalize(after, gain_ref[2:3], shift_ref[2:3])
        inner = jnp.maximum(matmul(normed, first_ref[...]) + first_offset_ref[...], 0.0).astype(
            jnp.bfloat16
        )
        final = after + (matmul(inner, second_ref[...]) + second_offset_ref[...])
        for item in range(group):
            for tile in range(final_ref.shape[0]):
                final_ref.at[tile][pl.ds(start // seqs + item, seqs, stride=residues), :] = final[
                    item * seqs : (item + 1) * seqs, tile * LANES : (tile + 1) * LANES
                ]
    for tile in range(final_ref.shape[0]):
        out_ref[:, tile * LANES : (tile + 1) * LANES] = final_ref[tile]


def call(kernel, out_shape, scratch=(), flops=0, transcendentals=0, name=None):
    return pl.pallas_call(
        kernel,
        out_shape=out_shape,
        scratch_shapes=list(scratch),
        compiler_params=pltpu.CompilerParams(vmem_limit_bytes=VMEM_LIMIT),
        cost_estimate=pl.CostEstimate(
            flops=flops, bytes_accessed=2**21, transcendentals=transcendentals
        ),
        name=name,
    )


def attention(normed, entry, gate_offset):
    rows, channels = normed.shape
    return call(
        attention_kernel,
        jax.ShapeDtypeStruct((rows, channels), jnp.bfloat16),
        [pltpu.VMEM((rows, channels), jnp.bfloat16)] * 3 + [pltpu.VMEM((rows, channels), jnp.float32)],
        flops=8 * rows * channels * channels + 4 * rows * rows * channels,
        transcendentals=HEADS * rows * rows,
        name="attention",
    )(normed, entry, gate_offset.reshape(1, channels))


def exchange(values, axis):
    count = lax.axis_size(axis)
    rows, channels = values.shape
    return lax.all_to_all(
        values.reshape(count, rows // count, channels), axis, split_axis=0, concat_axis=0, tiled=True
    ).reshape(rows, channels)


def shards(
    alignment_tensor,
    standardizer_factors,
    standardizer_offsets,
    horizontal_entry_matrix,
    horizontal_sigmoid_offset,
    horizontal_exit_matrix,
    horizontal_exit_offset,
    vertical_entry_matrix,
    vertical_sigmoid_offset,
    vertical_exit_matrix,
    vertical_exit_offset,
    feedforward_first_matrix,
    feedforward_first_offset,
    feedforward_second_matrix,
    feedforward_second_offset,
):
    seq_local, res_local, channels = alignment_tensor.shape
    rows = seq_local * res_local
    base = alignment_tensor.reshape(rows, channels)
    narrow = jax.ShapeDtypeStruct((rows, channels), jnp.bfloat16)
    wide = jax.ShapeDtypeStruct((rows, channels), jnp.float32)
    row_normed = call(norm_kernel, narrow, name="row_norm")(
        base, standardizer_factors, standardizer_offsets
    )
    row_gated = attention(
        exchange(row_normed, "res"), horizontal_entry_matrix, horizontal_sigmoid_offset
    )
    after_row, col_normed = call(
        functools.partial(turn_kernel, res_local),
        (wide, narrow),
        [pltpu.VMEM((channels // LANES, rows, LANES), jnp.float32)],
        flops=2 * rows * channels * channels,
        name="after_row",
    )(
        base,
        exchange(row_gated, "res"),
        horizontal_exit_matrix,
        horizontal_exit_offset.reshape(1, channels),
        standardizer_factors,
        standardizer_offsets,
    )
    col_gated = attention(exchange(col_normed, "seq"), vertical_entry_matrix, vertical_sigmoid_offset)
    updated = call(
        functools.partial(transition_kernel, res_local),
        wide,
        [pltpu.VMEM((channels // LANES, rows, LANES), jnp.float32)],
        flops=18 * rows * channels * channels,
        name="transition",
    )(
        after_row,
        exchange(col_gated, "seq"),
        vertical_exit_matrix,
        vertical_exit_offset.reshape(1, channels),
        standardizer_factors,
        standardizer_offsets,
        feedforward_first_matrix,
        feedforward_first_offset.reshape(1, -1),
        feedforward_second_matrix,
        feedforward_second_offset.reshape(1, channels),
    )
    return updated.reshape(seq_local, res_local, channels)


def solution(mesh):
    return jax.shard_map(
        shards,
        mesh=mesh,
        in_specs=(P("seq", "res", None),) + (P(),) * 14,
        out_specs=P("seq", "res", None),
        check_vma=False,
    )
```

```python
import functools

import jax
import jax.numpy as jnp
from jax import lax
from jax.experimental import pallas as pl
from jax.experimental.pallas import tpu as pltpu
from jax.sharding import Mesh
from jax.sharding import PartitionSpec as P

HEADS = 8
CORES = 2
LANES = 128
BLOCK = 256
EPSILON = 1e-05
LOG2E = 1.4426950408889634
VMEM_LIMIT = 48 * 1024 * 1024
WHOLE_VMEM = 63 * 1024 * 1024

GAIN, SHIFT, ROW_GATE, ROW_EXIT, COL_GATE, COL_EXIT, SECOND, FIRST = 0, 3, 6, 7, 8, 9, 10, 12
PACKED = 16


def normalize(values, gain, shift):
    row_mean = jnp.mean(values, axis=-1, keepdims=True)
    centred = values - row_mean
    variance = jnp.mean(centred * centred, axis=-1, keepdims=True)
    return (centred * lax.rsqrt(variance + EPSILON) * gain + shift).astype(jnp.bfloat16)


def matmul(left, right):
    return jnp.dot(left, right, preferred_element_type=jnp.float32)


def centre_kernel(*refs):
    places = (GAIN, SHIFT, ROW_GATE, ROW_EXIT, COL_GATE, COL_EXIT, SECOND, FIRST)
    small = len(places)
    base_hbm, small_hbm = refs[0], refs[1 : 1 + small]
    out_ref, packed_ref, base_ref = refs[1 + small : 4 + small]
    small_refs, base_sem, small_sem = refs[4 + small : 4 + 2 * small], refs[-2], refs[-1]
    rows, channels = base_ref.shape
    parts = base_sem.shape[0]
    part = rows // parts
    copies = [
        pltpu.make_async_copy(
            base_hbm.at[pl.ds(i * part, part)], base_ref.at[pl.ds(i * part, part)], base_sem.at[i]
        )
        for i in range(parts)
    ]
    for copy in copies:
        copy.start()
    small_copies = [
        pltpu.make_async_copy(small_hbm[i], small_refs[i], small_sem.at[i]) for i in range(small)
    ]
    for copy in small_copies:
        copy.start()
    for i in range(parts):
        copies[i].wait()
        values = base_ref[i * part : (i + 1) * part]
        out_ref[i * part : (i + 1) * part] = (
            values - jnp.mean(values, axis=-1, keepdims=True)
        ).astype(jnp.bfloat16)
    packed_ref[...] = jnp.zeros_like(packed_ref)
    for i, place in enumerate(places):
        small_copies[i].wait()
        count, width = small_refs[i].shape
        for j in range(count):
            for k in range(width // channels):
                row = place + j + k
                packed_ref[row : row + 1] = small_refs[i][j : j + 1, k * channels : (k + 1) * channels]


def project(normed, entry_ref, gate, query_ref, key_ref, value_ref, gate_ref):
    channels = normed.shape[1]
    scale = LOG2E * (channels // HEADS) ** -0.5
    query_ref[...] = (matmul(normed, entry_ref[:, :channels]) * scale).astype(jnp.bfloat16)
    key_ref[...] = matmul(normed, entry_ref[:, channels : 2 * channels]).astype(jnp.bfloat16)
    value = matmul(normed, entry_ref[:, 2 * channels : 3 * channels]).astype(jnp.bfloat16)
    for tile in range(channels // LANES):
        value_ref[tile, :, :LANES] = value[:, tile * LANES : (tile + 1) * LANES]
        value_ref[tile, :, LANES:] = jnp.ones((normed.shape[0], LANES), jnp.bfloat16)
    gate_ref[...] = jax.nn.sigmoid(matmul(normed, entry_ref[:, 3 * channels :]) + gate)


def attend(span, query_ref, key_ref, value_ref, gate_ref):
    channels = query_ref.shape[1]
    head_size = channels // HEADS
    lane_head = lax.broadcasted_iota(jnp.int32, (1, LANES), 1) // head_size
    gated = []
    for tile in range(channels // LANES):
        lanes = slice(tile * LANES, (tile + 1) * LANES)
        queries = query_ref[span, lanes]
        keys = key_ref[:, lanes]
        mixed = jnp.zeros(queries.shape, jnp.float32)
        for head in range(LANES // head_size):
            mask = (lane_head == head).astype(jnp.float32)
            scores = lax.dot_general(
                queries * mask.astype(jnp.bfloat16),
                keys,
                (((1,), (1,)), ((), ())),
                preferred_element_type=jnp.float32,
            )
            peak = jnp.max(scores, axis=-1, keepdims=True)
            weights = jnp.exp2(scores - peak).astype(jnp.bfloat16)
            result = matmul(weights, value_ref[tile])
            mixed = jnp.where(lane_head == head, result[:, :LANES] / result[:, LANES:], mixed)
        gated.append((gate_ref[span, lanes] * mixed).astype(jnp.bfloat16))
    return jnp.concatenate(gated, axis=1)


def row_kernel(
    columns, residual_ref, entry_ref, exit_ref, packed_ref, out_ref, query_ref, key_ref, value_ref, gate_ref, after_ref
):
    rows = residual_ref.shape[0]
    normed = normalize(
        residual_ref[...].astype(jnp.float32), packed_ref[GAIN : GAIN + 1], packed_ref[SHIFT : SHIFT + 1]
    )
    work = (query_ref, key_ref, value_ref, gate_ref)
    project(normed, entry_ref, packed_ref[ROW_GATE : ROW_GATE + 1], *work)
    tiles = range(after_ref.shape[0])
    for start in range(0, rows, BLOCK):
        span = slice(start, min(start + BLOCK, rows))
        after = residual_ref[span, :].astype(jnp.float32) + (
            matmul(attend(span, *work), exit_ref[...]) + packed_ref[ROW_EXIT : ROW_EXIT + 1]
        )
        for tile in tiles:
            after_ref[tile, span, :] = after[:, tile * LANES : (tile + 1) * LANES]
    stride = CORES * columns
    chips = rows // stride
    pair = 2
    for first in range(0, stride, pair):
        for tile in tiles:
            picked = [
                after_ref.at[tile][pl.ds(first + i, chips, stride=stride), :] for i in range(pair)
            ]
            out_ref[first * chips : (first + pair) * chips, tile * LANES : (tile + 1) * LANES] = (
                jnp.concatenate(picked, axis=0).astype(jnp.bfloat16)
            )


def interleave_kernel(values_ref, out_ref, mixed_ref):
    rows = values_ref.shape[0]
    half = rows // CORES
    for tile in range(mixed_ref.shape[0]):
        lanes = slice(tile * LANES, (tile + 1) * LANES)
        for core in range(CORES):
            mixed_ref.at[tile][pl.ds(core, half, stride=CORES), :] = values_ref[
                core * half : (core + 1) * half, lanes
            ].astype(jnp.float32)
        out_ref[:, lanes] = mixed_ref[tile].astype(jnp.bfloat16)


def col_kernel(
    residual_ref,
    entry_ref,
    exit_ref,
    first_ref,
    second_ref,
    packed_ref,
    out_ref,
    query_ref,
    key_ref,
    value_ref,
    gate_ref,
):
    rows, channels = residual_ref.shape
    normed = normalize(
        residual_ref[...].astype(jnp.float32),
        packed_ref[GAIN + 1 : GAIN + 2],
        packed_ref[SHIFT + 1 : SHIFT + 2],
    )
    work = (query_ref, key_ref, value_ref, gate_ref)
    project(normed, entry_ref, packed_ref[COL_GATE : COL_GATE + 1], *work)
    for start in range(0, rows, BLOCK):
        span = slice(start, min(start + BLOCK, rows))
        after = residual_ref[span, :].astype(jnp.float32) + (
            matmul(attend(span, *work), exit_ref[...]) + packed_ref[COL_EXIT : COL_EXIT + 1]
        )
        normed = normalize(after, packed_ref[GAIN + 2 : GAIN + 3], packed_ref[SHIFT + 2 : SHIFT + 3])
        update = packed_ref[SECOND : SECOND + 1]
        for part in range(first_ref.shape[1] // channels):
            hidden = slice(part * channels, (part + 1) * channels)
            inner = jnp.maximum(
                matmul(normed, first_ref[:, hidden]) + packed_ref[FIRST + part : FIRST + part + 1], 0.0
            )
            update = update + matmul(inner.astype(jnp.bfloat16), second_ref[hidden, :])
        out_ref[span, :] = (after + update).astype(jnp.bfloat16)


def home_kernel(residues, base_ref, values_ref, out_ref, turned_ref):
    rows = base_ref.shape[0]
    seqs = rows // residues
    for tile in range(turned_ref.shape[0]):
        lanes = slice(tile * LANES, (tile + 1) * LANES)
        for item in range(residues):
            turned_ref.at[tile][pl.ds(item, seqs, stride=residues), :] = values_ref[
                item * seqs : (item + 1) * seqs, lanes
            ].astype(jnp.float32)
    mean = jnp.mean(base_ref[...], axis=-1, keepdims=True)
    for tile in range(turned_ref.shape[0]):
        out_ref[:, tile * LANES : (tile + 1) * LANES] = turned_ref[tile] + mean


def call(
    kernel, out_shape, scratch=(), flops=0, transcendentals=0, name=None, vmem=VMEM_LIMIT, **specs
):
    return pl.pallas_call(
        kernel,
        out_shape=out_shape,
        scratch_shapes=list(scratch),
        compiler_params=pltpu.CompilerParams(vmem_limit_bytes=vmem),
        cost_estimate=pl.CostEstimate(
            flops=flops, bytes_accessed=2**21, transcendentals=transcendentals
        ),
        name=name,
        **specs,
    )


def exchange(values, axes):
    count = lax.axis_size(axes)
    rows, channels = values.shape
    return lax.all_to_all(
        values.reshape(count, rows // count, channels), axes, split_axis=0, concat_axis=0, tiled=True
    ).reshape(rows, channels)


def shards(
    alignment_tensor,
    standardizer_factors,
    standardizer_offsets,
    horizontal_entry_matrix,
    horizontal_sigmoid_offset,
    horizontal_exit_matrix,
    horizontal_exit_offset,
    vertical_entry_matrix,
    vertical_sigmoid_offset,
    vertical_exit_matrix,
    vertical_exit_offset,
    feedforward_first_matrix,
    feedforward_first_offset,
    feedforward_second_matrix,
    feedforward_second_offset,
):
    seq_local, res_local, channels = alignment_tensor.shape
    rows = seq_local * res_local
    base = alignment_tensor.reshape(rows, channels)
    narrow = jax.ShapeDtypeStruct((rows, channels), jnp.bfloat16)
    wide = jax.ShapeDtypeStruct((rows, channels), jnp.float32)
    split = pltpu.VMEM((channels // LANES, rows, LANES), jnp.float32)
    work = [
        pltpu.VMEM((rows, channels), jnp.bfloat16),
        pltpu.VMEM((rows, channels), jnp.bfloat16),
        pltpu.VMEM((channels // LANES, rows, 2 * LANES), jnp.bfloat16),
        pltpu.VMEM((rows, channels), jnp.float32),
    ]
    exps = HEADS * rows * rows
    attention_flops = 10 * rows * channels * channels + 4 * rows * rows * channels
    small = [
        standardizer_factors,
        standardizer_offsets,
        horizontal_sigmoid_offset.reshape(1, -1),
        horizontal_exit_offset.reshape(1, -1),
        vertical_sigmoid_offset.reshape(1, -1),
        vertical_exit_offset.reshape(1, -1),
        feedforward_second_offset.reshape(1, -1),
        feedforward_first_offset.reshape(1, -1),
    ]
    vmem = pl.BlockSpec(memory_space=pltpu.VMEM)
    centred, packed = call(
        centre_kernel,
        (narrow, jax.ShapeDtypeStruct((PACKED, channels), jnp.float32)),
        [pltpu.VMEM((rows, channels), jnp.float32)]
        + [pltpu.VMEM(array.shape, jnp.float32) for array in small]
        + [pltpu.SemaphoreType.DMA((4,)), pltpu.SemaphoreType.DMA((len(small),))],
        name="centre",
        vmem=WHOLE_VMEM,
        in_specs=[pl.BlockSpec(memory_space=pltpu.HBM)] * (1 + len(small)),
        out_specs=(vmem, vmem),
    )(base, *small)
    after_row = call(
        functools.partial(row_kernel, res_local),
        narrow,
        work + [split],
        flops=attention_flops,
        transcendentals=exps,
        name="row_attention",
    )(
        exchange(centred, ("chip", "core")),
        horizontal_entry_matrix,
        horizontal_exit_matrix,
        packed,
    )
    by_chip = call(interleave_kernel, narrow, [split], name="interleave")(exchange(after_row, "core"))
    updated = call(
        col_kernel,
        narrow,
        work,
        flops=attention_flops + 16 * rows * channels * channels,
        transcendentals=exps,
        name="col_attention_transition",
    )(
        exchange(by_chip, ("seq", "chip")),
        vertical_entry_matrix,
        vertical_exit_matrix,
        feedforward_first_matrix,
        feedforward_second_matrix,
        packed,
    )
    home = call(functools.partial(home_kernel, res_local), wide, [split], name="home")(
        base, exchange(updated, "seq")
    )
    return home.reshape(seq_local, res_local, channels)


def solution(mesh):
    seq_count, res_count = mesh.devices.shape
    cut = Mesh(mesh.devices.reshape(seq_count, res_count // CORES, CORES), ("seq", "chip", "core"))
    placed = P("seq", ("chip", "core"), None)
    return jax.shard_map(
        shards, mesh=cut, in_specs=(placed,) + (P(),) * 14, out_specs=placed, check_vma=False
    )
```

```python
import functools

import jax
import jax.numpy as jnp
from jax import lax
from jax.experimental import pallas as pl
from jax.experimental.pallas import tpu as pltpu
from jax.sharding import Mesh
from jax.sharding import PartitionSpec as P

HEADS = 8
X, Z_LOW, Z_HIGH, CORES = 4, 4, 3, 2
LANES = 128
PROJECT_ROWS, QUERY_ROWS = 256, 768
EPSILON = 1e-05
LOG2E = 1.4426950408889634
VMEM_LIMIT = 48 * 1024 * 1024
WHOLE_VMEM = 63 * 1024 * 1024

SEQ = ("x", "z_low")

GAIN, SHIFT, ROW_GATE, ROW_EXIT, COL_GATE, COL_EXIT, SECOND, FIRST = 0, 3, 6, 7, 8, 9, 10, 12
PACKED = 16


def normalize(values, gain, shift):
    row_mean = jnp.mean(values, axis=-1, keepdims=True)
    centred = values - row_mean
    variance = jnp.mean(centred * centred, axis=-1, keepdims=True)
    return (centred * lax.rsqrt(variance + EPSILON) * gain + shift).astype(jnp.bfloat16)


def matmul(left, right):
    return jnp.dot(left, right, preferred_element_type=jnp.float32)


def by_device(block):
    y, rest = divmod(block, Z_HIGH * CORES)
    z_high, core = divmod(rest, CORES)
    return (y * CORES + core) * Z_HIGH + z_high


def centre_kernel(columns, *refs):
    places = (GAIN, SHIFT, ROW_GATE, ROW_EXIT, COL_GATE, COL_EXIT, SECOND, FIRST)
    small = len(places)
    base_hbm, small_hbm = refs[0], refs[1 : 1 + small]
    out_hbm, packed_ref, base_ref, out_ref = refs[1 + small : 5 + small]
    small_refs, (base_sem, out_sem, small_sem) = refs[5 + small : 5 + 2 * small], refs[-3:]
    rows, channels = base_ref.shape
    parts = base_sem.shape[0]
    part = rows // parts
    assert part % (columns * Z_HIGH * CORES) == 0
    copies = [
        pltpu.make_async_copy(
            base_hbm.at[pl.ds(i * part, part)], base_ref.at[pl.ds(i * part, part)], base_sem.at[i]
        )
        for i in range(parts)
    ]
    for copy in copies:
        copy.start()
    small_copies = [
        pltpu.make_async_copy(small_hbm[i], small_refs[i], small_sem.at[i]) for i in range(small)
    ]
    for copy in small_copies:
        copy.start()
    out_copies = [
        pltpu.make_async_copy(
            out_ref.at[pl.ds(i * part, part)], out_hbm.at[pl.ds(i * part, part)], out_sem.at[i]
        )
        for i in range(parts)
    ]
    for i in range(parts):
        copies[i].wait()
        values = base_ref[i * part : (i + 1) * part]
        centred = (values - jnp.mean(values, axis=-1, keepdims=True)).astype(jnp.bfloat16)
        for first in range(0, part, columns):
            place = by_device((i * part + first) // columns) * columns
            out_ref[place : place + columns] = centred[first : first + columns]
        out_copies[i].start()
    packed_ref[...] = jnp.zeros_like(packed_ref)
    for i, place in enumerate(places):
        small_copies[i].wait()
        count, width = small_refs[i].shape
        for j in range(count):
            for k in range(width // channels):
                row = place + j + k
                packed_ref[row : row + 1] = small_refs[i][j : j + 1, k * channels : (k + 1) * channels]
    for copy in out_copies:
        copy.wait()


def spans(rows, block):
    return [slice(start, min(start + block, rows)) for start in range(0, rows, block)]


def project(residual_ref, entry_ref, gain, shift, gate, query_ref, key_ref, value_ref, gate_ref):
    rows, channels = residual_ref.shape
    scale = LOG2E * (channels // HEADS) ** -0.5
    for span in spans(rows, PROJECT_ROWS):
        normed = normalize(residual_ref[span, :].astype(jnp.float32), gain, shift)
        query_ref[span, :] = (matmul(normed, entry_ref[:, :channels]) * scale).astype(jnp.bfloat16)
        key_ref[span, :] = matmul(normed, entry_ref[:, channels : 2 * channels]).astype(jnp.bfloat16)
        value = matmul(normed, entry_ref[:, 2 * channels : 3 * channels]).astype(jnp.bfloat16)
        for tile in range(channels // LANES):
            value_ref[tile, span, :LANES] = value[:, tile * LANES : (tile + 1) * LANES]
            value_ref[tile, span, LANES:] = jnp.ones((normed.shape[0], LANES), jnp.bfloat16)
        gate_ref[span, :] = jax.nn.sigmoid(matmul(normed, entry_ref[:, 3 * channels :]) + gate)


def attend(span, query_ref, key_ref, value_ref, gate_ref):
    channels = query_ref.shape[1]
    head_size = channels // HEADS
    lane_head = lax.broadcasted_iota(jnp.int32, (1, LANES), 1) // head_size
    gated = []
    for tile in range(channels // LANES):
        lanes = slice(tile * LANES, (tile + 1) * LANES)
        queries = query_ref[span, lanes]
        keys = key_ref[:, lanes]
        mixed = jnp.zeros(queries.shape, jnp.float32)
        for head in range(LANES // head_size):
            mask = (lane_head == head).astype(jnp.float32)
            scores = lax.dot_general(
                queries * mask.astype(jnp.bfloat16),
                keys,
                (((1,), (1,)), ((), ())),
                preferred_element_type=jnp.float32,
            )
            peak = jnp.max(scores, axis=-1, keepdims=True)
            weights = jnp.exp2(scores - peak).astype(jnp.bfloat16)
            result = matmul(weights, value_ref[tile])
            mixed = jnp.where(lane_head == head, result[:, :LANES] / result[:, LANES:], mixed)
        gated.append((gate_ref[span, lanes] * mixed).astype(jnp.bfloat16))
    return jnp.concatenate(gated, axis=1)


def row_kernel(columns, residual_ref, entry_ref, exit_ref, packed_ref, out_ref, *work):
    rows = residual_ref.shape[0]
    project(
        residual_ref,
        entry_ref,
        packed_ref[GAIN : GAIN + 1],
        packed_ref[SHIFT : SHIFT + 1],
        packed_ref[ROW_GATE : ROW_GATE + 1],
        *work,
    )
    for span in spans(rows, QUERY_ROWS):
        after = residual_ref[span, :].astype(jnp.float32) + (
            matmul(attend(span, *work), exit_ref[...]) + packed_ref[ROW_EXIT : ROW_EXIT + 1]
        )
        after = after.astype(jnp.bfloat16)
        for first in range(span.start, span.stop, columns):
            y, rest = divmod(first // columns, CORES * Z_HIGH)
            core, z_high = divmod(rest, Z_HIGH)
            place = core * (rows // CORES) + (y * Z_HIGH + z_high) * columns
            out_ref[place : place + columns, :] = after[first - span.start : first - span.start + columns]


def turn_kernel(columns, values_ref, *refs):
    out_ref, turned_ref = refs[-2:]
    rows = values_ref.shape[0]
    half = rows // CORES
    chips = half // columns
    for tile in range(turned_ref.shape[0]):
        lanes = slice(tile * LANES, (tile + 1) * LANES)
        for core in range(CORES):
            values = values_ref[core * half : (core + 1) * half, lanes].astype(jnp.float32)
            for chip in range(chips):
                turned_ref.at[tile][pl.ds(chip * CORES + core, columns, stride=CORES * chips), :] = (
                    values[chip * columns : (chip + 1) * columns]
                )
        out_ref[:, lanes] = turned_ref[tile].astype(jnp.bfloat16)


def col_kernel(residual_ref, entry_ref, exit_ref, first_ref, second_ref, packed_ref, out_ref, *work):
    rows, channels = residual_ref.shape
    project(
        residual_ref,
        entry_ref,
        packed_ref[GAIN + 1 : GAIN + 2],
        packed_ref[SHIFT + 1 : SHIFT + 2],
        packed_ref[COL_GATE : COL_GATE + 1],
        *work,
    )
    for span in spans(rows, QUERY_ROWS):
        after = residual_ref[span, :].astype(jnp.float32) + (
            matmul(attend(span, *work), exit_ref[...]) + packed_ref[COL_EXIT : COL_EXIT + 1]
        )
        normed = normalize(after, packed_ref[GAIN + 2 : GAIN + 3], packed_ref[SHIFT + 2 : SHIFT + 3])
        update = packed_ref[SECOND : SECOND + 1]
        for part in range(first_ref.shape[1] // channels):
            hidden = slice(part * channels, (part + 1) * channels)
            inner = jnp.maximum(
                matmul(normed, first_ref[:, hidden]) + packed_ref[FIRST + part : FIRST + part + 1], 0.0
            )
            update = update + matmul(inner.astype(jnp.bfloat16), second_ref[hidden, :])
        out_ref[span, :] = (after + update).astype(jnp.bfloat16)


def home_kernel(residues, base_ref, values_ref, out_ref, turned_ref):
    rows = base_ref.shape[0]
    seqs = rows // residues
    for tile in range(turned_ref.shape[0]):
        lanes = slice(tile * LANES, (tile + 1) * LANES)
        for item in range(residues):
            turned_ref.at[tile][pl.ds(item, seqs, stride=residues), :] = values_ref[
                item * seqs : (item + 1) * seqs, lanes
            ].astype(jnp.float32)
    mean = jnp.mean(base_ref[...], axis=-1, keepdims=True)
    for tile in range(turned_ref.shape[0]):
        out_ref[:, tile * LANES : (tile + 1) * LANES] = turned_ref[tile] + mean


def call(
    kernel, out_shape, scratch=(), flops=0, transcendentals=0, name=None, vmem=VMEM_LIMIT, **specs
):
    return pl.pallas_call(
        kernel,
        out_shape=out_shape,
        scratch_shapes=list(scratch),
        compiler_params=pltpu.CompilerParams(vmem_limit_bytes=vmem),
        cost_estimate=pl.CostEstimate(
            flops=flops, bytes_accessed=2**21, transcendentals=transcendentals
        ),
        name=name,
        **specs,
    )


def exchange(values, axes):
    count = lax.axis_size(axes)
    rows, channels = values.shape
    return lax.all_to_all(
        values.reshape(count, rows // count, channels), axes, split_axis=0, concat_axis=0, tiled=True
    ).reshape(rows, channels)


def shards(
    alignment_tensor,
    standardizer_factors,
    standardizer_offsets,
    horizontal_entry_matrix,
    horizontal_sigmoid_offset,
    horizontal_exit_matrix,
    horizontal_exit_offset,
    vertical_entry_matrix,
    vertical_sigmoid_offset,
    vertical_exit_matrix,
    vertical_exit_offset,
    feedforward_first_matrix,
    feedforward_first_offset,
    feedforward_second_matrix,
    feedforward_second_offset,
):
    seq_local, res_local, channels = alignment_tensor.shape
    rows = seq_local * res_local
    seq_count = lax.axis_size(SEQ)
    base = alignment_tensor.reshape(rows, channels)
    narrow = jax.ShapeDtypeStruct((rows, channels), jnp.bfloat16)
    wide = jax.ShapeDtypeStruct((rows, channels), jnp.float32)
    split = pltpu.VMEM((channels // LANES, rows, LANES), jnp.float32)
    work = [
        pltpu.VMEM((rows, channels), jnp.bfloat16),
        pltpu.VMEM((rows, channels), jnp.bfloat16),
        pltpu.VMEM((channels // LANES, rows, 2 * LANES), jnp.bfloat16),
        pltpu.VMEM((rows, channels), jnp.float32),
    ]
    exps = HEADS * rows * rows
    attention_flops = 10 * rows * channels * channels + 4 * rows * rows * channels
    small = [
        standardizer_factors,
        standardizer_offsets,
        horizontal_sigmoid_offset.reshape(1, -1),
        horizontal_exit_offset.reshape(1, -1),
        vertical_sigmoid_offset.reshape(1, -1),
        vertical_exit_offset.reshape(1, -1),
        feedforward_second_offset.reshape(1, -1),
        feedforward_first_offset.reshape(1, -1),
    ]
    parts = max(rows // (2 * seq_count * Z_HIGH * CORES), 1)
    vmem = pl.BlockSpec(memory_space=pltpu.VMEM)
    hbm = pl.BlockSpec(memory_space=pltpu.HBM)
    centred, packed = call(
        functools.partial(centre_kernel, seq_count),
        (narrow, jax.ShapeDtypeStruct((PACKED, channels), jnp.float32)),
        [pltpu.VMEM((rows, channels), jnp.float32), pltpu.VMEM((rows, channels), jnp.bfloat16)]
        + [pltpu.VMEM(array.shape, jnp.float32) for array in small]
        + [pltpu.SemaphoreType.DMA((count,)) for count in (parts, parts, len(small))],
        name="centre",
        vmem=WHOLE_VMEM,
        in_specs=[hbm] * (1 + len(small)),
        out_specs=(hbm, vmem),
    )(base, *small)
    after_row = call(
        functools.partial(row_kernel, seq_count),
        narrow,
        work,
        flops=attention_flops,
        transcendentals=exps,
        name="row_attention",
    )(
        exchange(centred, ("y", "core", "z_high")),
        horizontal_entry_matrix,
        horizontal_exit_matrix,
        packed,
    )
    col_weights = (
        vertical_entry_matrix,
        vertical_exit_matrix,
        feedforward_first_matrix,
        feedforward_second_matrix,
    )
    by_chip = call(functools.partial(turn_kernel, seq_count), narrow, [split], name="turn")(
        exchange(after_row, "core"), *col_weights
    )
    updated = call(
        col_kernel,
        narrow,
        work,
        flops=attention_flops + 16 * rows * channels * channels,
        transcendentals=exps,
        name="col_attention_transition",
    )(
        exchange(by_chip, SEQ + ("y", "z_high")),
        *col_weights,
        packed,
    )
    home = call(functools.partial(home_kernel, res_local), wide, [split], name="home")(
        base, exchange(updated, SEQ)
    )
    return home.reshape(seq_local, res_local, channels)


def solution(mesh):
    axes = ("z_low", "x", "z_high", "y", "core")
    cut = Mesh(mesh.devices.reshape(Z_LOW, X, Z_HIGH, -1, CORES), axes)
    placed = P(axes[:2], axes[2:], None)
    return jax.shard_map(
        shards, mesh=cut, in_specs=(placed,) + (P(),) * 14, out_specs=placed, check_vma=False
    )
```

```python
import functools

import jax
import jax.numpy as jnp
from jax import lax
from jax.experimental import pallas as pl
from jax.experimental.pallas import tpu as pltpu
from jax.sharding import Mesh
from jax.sharding import PartitionSpec as P

HEADS = 8
X, Z_LOW, Z_HIGH, CORES = 4, 4, 3, 2
LANES = 128
PROJECT_ROWS, QUERY_ROWS = 256, 768
EPSILON = 1e-05
LOG2E = 1.4426950408889634
VMEM_LIMIT = 48 * 1024 * 1024
WHOLE_VMEM = 63 * 1024 * 1024

SEQ = ("z_low", "x")

GAIN, SHIFT, ROW_GATE, ROW_EXIT, COL_GATE, COL_EXIT, SECOND, FIRST = 0, 3, 6, 7, 8, 9, 10, 12
PACKED = 16


def normalize(values, gain, shift):
    row_mean = jnp.mean(values, axis=-1, keepdims=True)
    centred = values - row_mean
    variance = jnp.mean(centred * centred, axis=-1, keepdims=True)
    return (centred * lax.rsqrt(variance + EPSILON) * gain + shift).astype(jnp.bfloat16)


def matmul(left, right):
    return jnp.dot(left, right, preferred_element_type=jnp.float32)


def by_device(block):
    y, rest = divmod(block, Z_HIGH * CORES)
    z_high, core = divmod(rest, CORES)
    return (y * CORES + core) * Z_HIGH + z_high


def centre_kernel(columns, *refs):
    places = (GAIN, SHIFT, ROW_GATE, ROW_EXIT, COL_GATE, COL_EXIT, SECOND, FIRST)
    small = len(places)
    base_hbm, small_hbm = refs[0], refs[1 : 1 + small]
    out_ref, packed_ref, base_ref = refs[1 + small : 4 + small]
    small_refs, (base_sem, small_sem) = refs[4 + small : 4 + 2 * small], refs[-2:]
    rows, channels = base_ref.shape
    parts = base_sem.shape[0]
    part = rows // parts
    assert part % (columns * Z_HIGH * CORES) == 0
    copies = [
        pltpu.make_async_copy(
            base_hbm.at[pl.ds(i * part, part)], base_ref.at[pl.ds(i * part, part)], base_sem.at[i]
        )
        for i in range(parts)
    ]
    for copy in copies:
        copy.start()
    small_copies = [
        pltpu.make_async_copy(small_hbm[i], small_refs[i], small_sem.at[i]) for i in range(small)
    ]
    for copy in small_copies:
        copy.start()
    for i in range(parts):
        copies[i].wait()
        values = base_ref[i * part : (i + 1) * part]
        centred = (values - jnp.mean(values, axis=-1, keepdims=True)).astype(jnp.bfloat16)
        for first in range(0, part, columns):
            place = by_device((i * part + first) // columns) * columns
            out_ref[place : place + columns] = centred[first : first + columns]
    packed_ref[...] = jnp.zeros_like(packed_ref)
    for i, place in enumerate(places):
        small_copies[i].wait()
        count, width = small_refs[i].shape
        for j in range(count):
            for k in range(width // channels):
                row = place + j + k
                packed_ref[row : row + 1] = small_refs[i][j : j + 1, k * channels : (k + 1) * channels]


def spans(rows, block):
    return [slice(start, min(start + block, rows)) for start in range(0, rows, block)]


def project(residual_ref, entry_ref, gain, shift, gate, query_ref, key_ref, value_ref, gate_ref):
    rows, channels = residual_ref.shape
    scale = LOG2E * (channels // HEADS) ** -0.5
    for span in spans(rows, PROJECT_ROWS):
        normed = normalize(residual_ref[span, :].astype(jnp.float32), gain, shift)
        query_ref[span, :] = (matmul(normed, entry_ref[:, :channels]) * scale).astype(jnp.bfloat16)
        key_ref[span, :] = matmul(normed, entry_ref[:, channels : 2 * channels]).astype(jnp.bfloat16)
        value = matmul(normed, entry_ref[:, 2 * channels : 3 * channels]).astype(jnp.bfloat16)
        for tile in range(channels // LANES):
            value_ref[tile, span, :LANES] = value[:, tile * LANES : (tile + 1) * LANES]
            value_ref[tile, span, LANES:] = jnp.ones((normed.shape[0], LANES), jnp.bfloat16)
        gate_ref[span, :] = jax.nn.sigmoid(matmul(normed, entry_ref[:, 3 * channels :]) + gate)


def attend(queries, gates, key_ref, value_ref):
    channels = queries.shape[1]
    head_size = channels // HEADS
    lane_head = lax.broadcasted_iota(jnp.int32, (1, LANES), 1) // head_size
    gated = []
    for tile in range(channels // LANES):
        lanes = slice(tile * LANES, (tile + 1) * LANES)
        keys = key_ref[:, lanes]
        mixed = jnp.zeros((queries.shape[0], LANES), jnp.float32)
        for head in range(LANES // head_size):
            mask = (lane_head == head).astype(jnp.float32)
            scores = lax.dot_general(
                queries[:, lanes] * mask.astype(jnp.bfloat16),
                keys,
                (((1,), (1,)), ((), ())),
                preferred_element_type=jnp.float32,
            )
            peak = jnp.max(scores, axis=-1, keepdims=True)
            weights = jnp.exp2(scores - peak).astype(jnp.bfloat16)
            result = matmul(weights, value_ref[tile])
            mixed = jnp.where(lane_head == head, result[:, :LANES] / result[:, LANES:], mixed)
        gated.append((gates[:, lanes] * mixed).astype(jnp.bfloat16))
    return jnp.concatenate(gated, axis=1)


def for_core(ref, columns, core):
    size = Z_HIGH * columns
    return jnp.concatenate(
        [
            ref[pl.ds(pl.multiple_of(first + core * size, columns), size), :]
            for first in range(0, ref.shape[0], CORES * size)
        ],
        axis=0,
    )


def after_row(columns, core, residual_ref, exit_ref, packed_ref, query_ref, key_ref, value_ref, gate_ref):
    gated = attend(
        for_core(query_ref, columns, core), for_core(gate_ref, columns, core), key_ref, value_ref
    )
    update = matmul(gated, exit_ref[...]) + packed_ref[ROW_EXIT : ROW_EXIT + 1]
    return (for_core(residual_ref, columns, core).astype(jnp.float32) + update).astype(jnp.bfloat16)


def row_send_kernel(columns, core_ref, residual_ref, entry_ref, exit_ref, packed_ref, out_ref, *work):
    project(
        residual_ref,
        entry_ref,
        packed_ref[GAIN : GAIN + 1],
        packed_ref[SHIFT : SHIFT + 1],
        packed_ref[ROW_GATE : ROW_GATE + 1],
        *work,
    )
    out_ref[...] = after_row(columns, 1 - core_ref[0], residual_ref, exit_ref, packed_ref, *work)


def row_keep_kernel(columns, core_ref, residual_ref, exit_ref, packed_ref, *refs):
    *work, out_ref = refs
    out_ref[...] = after_row(columns, core_ref[0], residual_ref, exit_ref, packed_ref, *work)


def turn_kernel(columns, core_ref, kept_ref, received_ref, *refs):
    out_ref, turned_ref = refs[-2:]
    half = kept_ref.shape[0]
    chips = half // columns
    own = jnp.full((1, LANES), core_ref[0], jnp.int32) == 0
    for tile in range(turned_ref.shape[0]):
        lanes = slice(tile * LANES, (tile + 1) * LANES)
        kept = kept_ref[:, lanes].astype(jnp.float32)
        received = received_ref[:, lanes].astype(jnp.float32)
        for core, values in enumerate(
            (jnp.where(own, kept, received), jnp.where(own, received, kept))
        ):
            for chip in range(chips):
                turned_ref.at[tile][pl.ds(chip * CORES + core, columns, stride=CORES * chips), :] = (
                    values[chip * columns : (chip + 1) * columns]
                )
        out_ref[:, lanes] = turned_ref[tile].astype(jnp.bfloat16)


def col_kernel(residual_ref, entry_ref, exit_ref, first_ref, second_ref, packed_ref, out_ref, *work):
    rows, channels = residual_ref.shape
    project(
        residual_ref,
        entry_ref,
        packed_ref[GAIN + 1 : GAIN + 2],
        packed_ref[SHIFT + 1 : SHIFT + 2],
        packed_ref[COL_GATE : COL_GATE + 1],
        *work,
    )
    query_ref, key_ref, value_ref, gate_ref = work
    for span in spans(rows, QUERY_ROWS):
        after = residual_ref[span, :].astype(jnp.float32) + (
            matmul(
                attend(query_ref[span, :], gate_ref[span, :], key_ref, value_ref), exit_ref[...]
            ) + packed_ref[COL_EXIT : COL_EXIT + 1]
        )
        normed = normalize(after, packed_ref[GAIN + 2 : GAIN + 3], packed_ref[SHIFT + 2 : SHIFT + 3])
        update = packed_ref[SECOND : SECOND + 1]
        for part in range(first_ref.shape[1] // channels):
            hidden = slice(part * channels, (part + 1) * channels)
            inner = jnp.maximum(
                matmul(normed, first_ref[:, hidden]) + packed_ref[FIRST + part : FIRST + part + 1], 0.0
            )
            update = update + matmul(inner.astype(jnp.bfloat16), second_ref[hidden, :])
        out_ref[span, :] = (after + update).astype(jnp.bfloat16)


def home_kernel(residues, base_ref, values_ref, out_ref, turned_ref):
    rows = base_ref.shape[0]
    seqs = rows // residues
    for tile in range(turned_ref.shape[0]):
        lanes = slice(tile * LANES, (tile + 1) * LANES)
        for item in range(residues):
            turned_ref.at[tile][pl.ds(item, seqs, stride=residues), :] = values_ref[
                item * seqs : (item + 1) * seqs, lanes
            ].astype(jnp.float32)
    mean = jnp.mean(base_ref[...], axis=-1, keepdims=True)
    for tile in range(turned_ref.shape[0]):
        out_ref[:, tile * LANES : (tile + 1) * LANES] = turned_ref[tile] + mean


def call(
    kernel, out_shape, scratch=(), flops=0, transcendentals=0, name=None, vmem=VMEM_LIMIT, **specs
):
    return pl.pallas_call(
        kernel,
        out_shape=out_shape,
        scratch_shapes=list(scratch),
        compiler_params=pltpu.CompilerParams(vmem_limit_bytes=vmem),
        cost_estimate=pl.CostEstimate(
            flops=flops, bytes_accessed=2**21, transcendentals=transcendentals
        ),
        name=name,
        **specs,
    )


def exchange(values, axes):
    count = lax.axis_size(axes)
    rows, channels = values.shape
    return lax.all_to_all(
        values.reshape(count, rows // count, channels), axes, split_axis=0, concat_axis=0, tiled=True
    ).reshape(rows, channels)


def shards(
    alignment_tensor,
    standardizer_factors,
    standardizer_offsets,
    horizontal_entry_matrix,
    horizontal_sigmoid_offset,
    horizontal_exit_matrix,
    horizontal_exit_offset,
    vertical_entry_matrix,
    vertical_sigmoid_offset,
    vertical_exit_matrix,
    vertical_exit_offset,
    feedforward_first_matrix,
    feedforward_first_offset,
    feedforward_second_matrix,
    feedforward_second_offset,
):
    seq_local, res_local, channels = alignment_tensor.shape
    rows = seq_local * res_local
    seq_count = lax.axis_size(SEQ)
    base = alignment_tensor.reshape(rows, channels)
    narrow = jax.ShapeDtypeStruct((rows, channels), jnp.bfloat16)
    wide = jax.ShapeDtypeStruct((rows, channels), jnp.float32)
    split = pltpu.VMEM((channels // LANES, rows, LANES), jnp.float32)
    work = [
        pltpu.VMEM((rows, channels), jnp.bfloat16),
        pltpu.VMEM((rows, channels), jnp.bfloat16),
        pltpu.VMEM((channels // LANES, rows, 2 * LANES), jnp.bfloat16),
        pltpu.VMEM((rows, channels), jnp.float32),
    ]
    exps = HEADS * rows * rows
    attention_flops = 10 * rows * channels * channels + 4 * rows * rows * channels
    small = [
        standardizer_factors,
        standardizer_offsets,
        horizontal_sigmoid_offset.reshape(1, -1),
        horizontal_exit_offset.reshape(1, -1),
        vertical_sigmoid_offset.reshape(1, -1),
        vertical_exit_offset.reshape(1, -1),
        feedforward_second_offset.reshape(1, -1),
        feedforward_first_offset.reshape(1, -1),
    ]
    parts = max(rows // (2 * seq_count * Z_HIGH * CORES), 1)
    vmem = pl.BlockSpec(memory_space=pltpu.VMEM)
    hbm = pl.BlockSpec(memory_space=pltpu.HBM)
    centred, packed = call(
        functools.partial(centre_kernel, seq_count),
        (narrow, jax.ShapeDtypeStruct((PACKED, channels), jnp.float32)),
        [pltpu.VMEM((rows, channels), jnp.float32)]
        + [pltpu.VMEM(array.shape, jnp.float32) for array in small]
        + [pltpu.SemaphoreType.DMA((count,)) for count in (parts, len(small))],
        name="centre",
        vmem=WHOLE_VMEM,
        in_specs=[hbm] * (1 + len(small)),
        out_specs=(vmem, vmem),
    )(base, *small)
    core = lax.axis_index("core").astype(jnp.int32).reshape(1)
    smem = pl.BlockSpec(memory_space=pltpu.SMEM)
    half = jax.ShapeDtypeStruct((rows // CORES, channels), jnp.bfloat16)
    residual = exchange(centred, ("y", "core", "z_high"))
    sent, *projected = call(
        functools.partial(row_send_kernel, seq_count),
        (half, *(jax.ShapeDtypeStruct(array.shape, array.dtype) for array in work)),
        flops=attention_flops // 2,
        transcendentals=exps // 2,
        name="row_attention_send",
        in_specs=[smem] + [vmem] * 4,
        out_specs=(vmem,) * 5,
    )(core, residual, horizontal_entry_matrix, horizontal_exit_matrix, packed)
    received = lax.ppermute(sent, "core", [(i, CORES - 1 - i) for i in range(CORES)])
    kept = call(
        functools.partial(row_keep_kernel, seq_count),
        half,
        flops=attention_flops // 2,
        transcendentals=exps // 2,
        name="row_attention_keep",
        in_specs=[smem] + [vmem] * 7,
        out_specs=vmem,
    )(core, residual, horizontal_exit_matrix, packed, *projected)
    col_weights = (
        vertical_entry_matrix,
        vertical_exit_matrix,
        feedforward_first_matrix,
        feedforward_second_matrix,
    )
    by_chip = call(
        functools.partial(turn_kernel, seq_count),
        narrow,
        [split],
        name="turn",
        in_specs=[smem] + [vmem] * 6,
        out_specs=vmem,
    )(core, kept, received, *col_weights)
    updated = call(
        col_kernel,
        narrow,
        work,
        flops=attention_flops + 16 * rows * channels * channels,
        transcendentals=exps,
        name="col_attention_transition",
    )(
        exchange(by_chip, SEQ + ("y", "z_high")),
        *col_weights,
        packed,
    )
    home = call(functools.partial(home_kernel, res_local), wide, [split], name="home")(
        base, exchange(updated, SEQ)
    )
    return home.reshape(seq_local, res_local, channels)


def solution(mesh):
    axes = ("z_low", "x", "z_high", "y", "core")
    cut = Mesh(mesh.devices.reshape(Z_LOW, X, Z_HIGH, -1, CORES), axes)
    placed = P(axes[:2], axes[2:], None)
    return jax.shard_map(
        shards, mesh=cut, in_specs=(placed,) + (P(),) * 14, out_specs=placed, check_vma=False
    )
```

```python
import functools

import jax
import jax.numpy as jnp
from jax import lax
from jax.experimental import pallas as pl
from jax.experimental.pallas import tpu as pltpu
from jax.sharding import Mesh
from jax.sharding import PartitionSpec as P

HEADS = 8
X, Z_LOW, Z_HIGH, CORES = 4, 4, 3, 2
LANES = 128
PROJECT_ROWS, QUERY_ROWS = 256, 768
EPSILON = 1e-05
LOG2E = 1.4426950408889634
VMEM_LIMIT = 48 * 1024 * 1024

SEQ = ("z_low", "x")

GAIN, SHIFT, ROW_GATE, ROW_EXIT, COL_GATE, COL_EXIT, SECOND, FIRST = 0, 3, 6, 7, 8, 9, 10, 12
PACKED = 16


def normalize(values, gain, shift):
    row_mean = jnp.mean(values, axis=-1, keepdims=True)
    centred = values - row_mean
    variance = jnp.mean(centred * centred, axis=-1, keepdims=True)
    return (centred * lax.rsqrt(variance + EPSILON) * gain + shift).astype(jnp.bfloat16)


def matmul(left, right):
    return jnp.dot(left, right, preferred_element_type=jnp.float32)


def by_device(block):
    y, rest = divmod(block, Z_HIGH * CORES)
    z_high, core = divmod(rest, CORES)
    return (y * CORES + core) * Z_HIGH + z_high


def centre_kernel(columns, base_ref, out_ref):
    values = base_ref[...]
    centred = (values - jnp.mean(values, axis=-1, keepdims=True)).astype(jnp.bfloat16)
    for block in range(base_ref.shape[0] // columns):
        place = by_device(block) * columns
        out_ref[place : place + columns] = centred[block * columns : (block + 1) * columns]


def pack_kernel(*refs):
    packed_ref = refs[-1]
    channels = packed_ref.shape[1]
    packed_ref[...] = jnp.zeros_like(packed_ref)
    places = (GAIN, SHIFT, ROW_GATE, ROW_EXIT, COL_GATE, COL_EXIT, SECOND, FIRST)
    for place, ref in zip(places, refs):
        count, width = ref.shape
        for j in range(count):
            for k in range(width // channels):
                row = place + j + k
                packed_ref[row : row + 1] = ref[j : j + 1, k * channels : (k + 1) * channels]


def spans(rows, block):
    return [slice(start, min(start + block, rows)) for start in range(0, rows, block)]


def project(residual_ref, entry_ref, gain, shift, gate, query_ref, key_ref, value_ref, gate_ref):
    rows, channels = residual_ref.shape
    scale = LOG2E * (channels // HEADS) ** -0.5
    for span in spans(rows, PROJECT_ROWS):
        normed = normalize(residual_ref[span, :].astype(jnp.float32), gain, shift)
        query_ref[span, :] = (matmul(normed, entry_ref[:, :channels]) * scale).astype(jnp.bfloat16)
        key_ref[span, :] = matmul(normed, entry_ref[:, channels : 2 * channels]).astype(jnp.bfloat16)
        value = matmul(normed, entry_ref[:, 2 * channels : 3 * channels]).astype(jnp.bfloat16)
        for tile in range(channels // LANES):
            value_ref[tile, span, :LANES] = value[:, tile * LANES : (tile + 1) * LANES]
            value_ref[tile, span, LANES:] = jnp.ones((normed.shape[0], LANES), jnp.bfloat16)
        gate_ref[span, :] = jax.nn.sigmoid(matmul(normed, entry_ref[:, 3 * channels :]) + gate)


def attend(queries, gates, key_ref, value_ref):
    channels = queries.shape[1]
    head_size = channels // HEADS
    per_tile = LANES // head_size
    lane_head = lax.broadcasted_iota(jnp.int32, (1, LANES), 1) // head_size

    def score(number):
        tile, head = divmod(number, per_tile)
        lanes = slice(tile * LANES, (tile + 1) * LANES)
        mask = (lane_head == head).astype(jnp.float32)
        return lax.dot_general(
            queries[:, lanes] * mask.astype(jnp.bfloat16),
            key_ref[:, lanes],
            (((1,), (1,)), ((), ())),
            preferred_element_type=jnp.float32,
        )

    gated = []
    following = score(0)
    for number in range(HEADS):
        scores = following
        if number + 1 < HEADS:
            following = score(number + 1)
        tile, head = divmod(number, per_tile)
        peak = jnp.max(scores, axis=-1, keepdims=True)
        weights = jnp.exp2(scores - peak).astype(jnp.bfloat16)
        result = matmul(weights, value_ref[tile])
        ratio = result[:, :LANES] / result[:, LANES:]
        mixed = ratio if head == 0 else jnp.where(lane_head == head, ratio, mixed)
        if head + 1 == per_tile:
            gates_here = gates[:, tile * LANES : (tile + 1) * LANES]
            gated.append((gates_here * mixed).astype(jnp.bfloat16))
    return jnp.concatenate(gated, axis=1)


def for_core(ref, columns, core):
    size = Z_HIGH * columns
    return jnp.concatenate(
        [
            ref[pl.ds(pl.multiple_of(first + core * size, columns), size), :]
            for first in range(0, ref.shape[0], CORES * size)
        ],
        axis=0,
    )


def after_row(columns, core, residual_ref, exit_ref, packed_ref, query_ref, key_ref, value_ref, gate_ref):
    gated = attend(
        for_core(query_ref, columns, core), for_core(gate_ref, columns, core), key_ref, value_ref
    )
    update = matmul(gated, exit_ref[...]) + packed_ref[ROW_EXIT : ROW_EXIT + 1]
    return (for_core(residual_ref, columns, core).astype(jnp.float32) + update).astype(jnp.bfloat16)


def row_send_kernel(columns, core_ref, residual_ref, entry_ref, exit_ref, packed_ref, out_ref, *work):
    project(
        residual_ref,
        entry_ref,
        packed_ref[GAIN : GAIN + 1],
        packed_ref[SHIFT : SHIFT + 1],
        packed_ref[ROW_GATE : ROW_GATE + 1],
        *work,
    )
    out_ref[...] = after_row(columns, 1 - core_ref[0], residual_ref, exit_ref, packed_ref, *work)


def row_keep_kernel(columns, core_ref, residual_ref, exit_ref, packed_ref, *refs):
    *work, out_ref = refs
    out_ref[...] = after_row(columns, core_ref[0], residual_ref, exit_ref, packed_ref, *work)


def turn_kernel(columns, core_ref, kept_ref, received_ref, *refs):
    out_ref, turned_ref = refs[-2:]
    half = kept_ref.shape[0]
    chips = half // columns
    own = jnp.full((1, LANES), core_ref[0], jnp.int32) == 0
    for tile in range(turned_ref.shape[0]):
        lanes = slice(tile * LANES, (tile + 1) * LANES)
        kept = kept_ref[:, lanes].astype(jnp.float32)
        received = received_ref[:, lanes].astype(jnp.float32)
        for core, values in enumerate(
            (jnp.where(own, kept, received), jnp.where(own, received, kept))
        ):
            for chip in range(chips):
                turned_ref.at[tile][pl.ds(chip * CORES + core, columns, stride=CORES * chips), :] = (
                    values[chip * columns : (chip + 1) * columns]
                )
        out_ref[:, lanes] = turned_ref[tile].astype(jnp.bfloat16)


def col_kernel(residual_ref, entry_ref, exit_ref, first_ref, second_ref, packed_ref, out_ref, *work):
    rows, channels = residual_ref.shape
    project(
        residual_ref,
        entry_ref,
        packed_ref[GAIN + 1 : GAIN + 2],
        packed_ref[SHIFT + 1 : SHIFT + 2],
        packed_ref[COL_GATE : COL_GATE + 1],
        *work,
    )
    query_ref, key_ref, value_ref, gate_ref = work
    for span in spans(rows, QUERY_ROWS):
        after = residual_ref[span, :].astype(jnp.float32) + (
            matmul(
                attend(query_ref[span, :], gate_ref[span, :], key_ref, value_ref), exit_ref[...]
            ) + packed_ref[COL_EXIT : COL_EXIT + 1]
        )
        normed = normalize(after, packed_ref[GAIN + 2 : GAIN + 3], packed_ref[SHIFT + 2 : SHIFT + 3])
        update = packed_ref[SECOND : SECOND + 1]
        for part in range(first_ref.shape[1] // channels):
            hidden = slice(part * channels, (part + 1) * channels)
            inner = jnp.maximum(
                matmul(normed, first_ref[:, hidden]) + packed_ref[FIRST + part : FIRST + part + 1], 0.0
            )
            update = update + matmul(inner.astype(jnp.bfloat16), second_ref[hidden, :])
        out_ref[span, :] = (after + update).astype(jnp.bfloat16)


def home_kernel(residues, base_ref, values_ref, out_ref, turned_ref):
    rows = base_ref.shape[0]
    seqs = rows // residues
    for tile in range(turned_ref.shape[0]):
        lanes = slice(tile * LANES, (tile + 1) * LANES)
        for item in range(residues):
            turned_ref.at[tile][pl.ds(item, seqs, stride=residues), :] = values_ref[
                item * seqs : (item + 1) * seqs, lanes
            ].astype(jnp.float32)
    mean = jnp.mean(base_ref[...], axis=-1, keepdims=True)
    for tile in range(turned_ref.shape[0]):
        out_ref[:, tile * LANES : (tile + 1) * LANES] = turned_ref[tile] + mean


def call(kernel, out_shape, scratch=(), flops=0, transcendentals=0, name=None, **specs):
    return pl.pallas_call(
        kernel,
        out_shape=out_shape,
        scratch_shapes=list(scratch),
        compiler_params=pltpu.CompilerParams(vmem_limit_bytes=VMEM_LIMIT),
        cost_estimate=pl.CostEstimate(
            flops=flops, bytes_accessed=2**21, transcendentals=transcendentals
        ),
        name=name,
        **specs,
    )


def exchange(values, axes):
    count = lax.axis_size(axes)
    rows, channels = values.shape
    return lax.all_to_all(
        values.reshape(count, rows // count, channels), axes, split_axis=0, concat_axis=0, tiled=True
    ).reshape(rows, channels)


def shards(
    alignment_tensor,
    standardizer_factors,
    standardizer_offsets,
    horizontal_entry_matrix,
    horizontal_sigmoid_offset,
    horizontal_exit_matrix,
    horizontal_exit_offset,
    vertical_entry_matrix,
    vertical_sigmoid_offset,
    vertical_exit_matrix,
    vertical_exit_offset,
    feedforward_first_matrix,
    feedforward_first_offset,
    feedforward_second_matrix,
    feedforward_second_offset,
):
    seq_local, res_local, channels = alignment_tensor.shape
    rows = seq_local * res_local
    seq_count = lax.axis_size(SEQ)
    base = alignment_tensor.reshape(rows, channels)
    narrow = jax.ShapeDtypeStruct((rows, channels), jnp.bfloat16)
    wide = jax.ShapeDtypeStruct((rows, channels), jnp.float32)
    split = pltpu.VMEM((channels // LANES, rows, LANES), jnp.float32)
    work = [
        pltpu.VMEM((rows, channels), jnp.bfloat16),
        pltpu.VMEM((rows, channels), jnp.bfloat16),
        pltpu.VMEM((channels // LANES, rows, 2 * LANES), jnp.bfloat16),
        pltpu.VMEM((rows, channels), jnp.float32),
    ]
    exps = HEADS * rows * rows
    attention_flops = 10 * rows * channels * channels + 4 * rows * rows * channels
    small = [
        standardizer_factors,
        standardizer_offsets,
        horizontal_sigmoid_offset.reshape(1, -1),
        horizontal_exit_offset.reshape(1, -1),
        vertical_sigmoid_offset.reshape(1, -1),
        vertical_exit_offset.reshape(1, -1),
        feedforward_second_offset.reshape(1, -1),
        feedforward_first_offset.reshape(1, -1),
    ]
    vmem = pl.BlockSpec(memory_space=pltpu.VMEM)
    packed = call(
        pack_kernel, jax.ShapeDtypeStruct((PACKED, channels), jnp.float32), name="pack"
    )(*small, horizontal_entry_matrix, horizontal_exit_matrix)
    centred = call(functools.partial(centre_kernel, seq_count), narrow, name="centre")(base)
    core = lax.axis_index("core").astype(jnp.int32).reshape(1)
    smem = pl.BlockSpec(memory_space=pltpu.SMEM)
    half = jax.ShapeDtypeStruct((rows // CORES, channels), jnp.bfloat16)
    residual = exchange(centred, ("y", "core", "z_high"))
    sent, *projected = call(
        functools.partial(row_send_kernel, seq_count),
        (half, *(jax.ShapeDtypeStruct(array.shape, array.dtype) for array in work)),
        flops=attention_flops // 2,
        transcendentals=exps // 2,
        name="row_attention_send",
        in_specs=[smem] + [vmem] * 4,
        out_specs=(vmem,) * 5,
    )(core, residual, horizontal_entry_matrix, horizontal_exit_matrix, packed)
    received = lax.ppermute(sent, "core", [(i, CORES - 1 - i) for i in range(CORES)])
    kept = call(
        functools.partial(row_keep_kernel, seq_count),
        half,
        flops=attention_flops // 2,
        transcendentals=exps // 2,
        name="row_attention_keep",
        in_specs=[smem] + [vmem] * 7,
        out_specs=vmem,
    )(core, residual, horizontal_exit_matrix, packed, *projected)
    col_weights = (
        vertical_entry_matrix,
        vertical_exit_matrix,
        feedforward_first_matrix,
        feedforward_second_matrix,
    )
    by_chip = call(
        functools.partial(turn_kernel, seq_count),
        narrow,
        [split],
        name="turn",
        in_specs=[smem] + [vmem] * 6,
        out_specs=vmem,
    )(core, kept, received, *col_weights)
    updated = call(
        col_kernel,
        narrow,
        work,
        flops=attention_flops + 16 * rows * channels * channels,
        transcendentals=exps,
        name="col_attention_transition",
    )(
        exchange(by_chip, SEQ + ("y", "z_high")),
        *col_weights,
        packed,
    )
    home = call(functools.partial(home_kernel, res_local), wide, [split], name="home")(
        base, exchange(updated, SEQ)
    )
    return home.reshape(seq_local, res_local, channels)


def solution(mesh):
    axes = ("z_low", "x", "z_high", "y", "core")
    cut = Mesh(mesh.devices.reshape(Z_LOW, X, Z_HIGH, -1, CORES), axes)
    placed = P(axes[:2], axes[2:], None)
    return jax.shard_map(
        shards, mesh=cut, in_specs=(placed,) + (P(),) * 14, out_specs=placed, check_vma=False
    )
```

```python
import functools

import jax
import jax.numpy as jnp
from jax import lax
from jax.experimental import pallas as pl
from jax.experimental.pallas import tpu as pltpu
from jax.sharding import Mesh
from jax.sharding import PartitionSpec as P

HEADS = 8
X, Z_LOW, Z_HIGH, CORES = 4, 4, 3, 2
LANES = 128
PROJECT_ROWS, QUERY_ROWS = 256, 768
EPSILON = 1e-05
LOG2E = 1.4426950408889634
VMEM_LIMIT = 48 * 1024 * 1024

SEQ = ("z_low", "x")

GAIN, SHIFT, ROW_GATE, ROW_EXIT, COL_GATE, COL_EXIT, SECOND, FIRST = 0, 3, 6, 7, 8, 9, 10, 12
PACKED = 16


def normalize(values, gain, shift):
    row_mean = jnp.mean(values, axis=-1, keepdims=True)
    centred = values - row_mean
    variance = jnp.mean(centred * centred, axis=-1, keepdims=True)
    return (centred * lax.rsqrt(variance + EPSILON) * gain + shift).astype(jnp.bfloat16)


def matmul(left, right):
    return jnp.dot(left, right, preferred_element_type=jnp.float32)


def by_device(block):
    y, rest = divmod(block, Z_HIGH * CORES)
    z_high, core = divmod(rest, CORES)
    return (y * CORES + core) * Z_HIGH + z_high


def centre_kernel(columns, base_ref, out_ref):
    values = base_ref[...]
    centred = (values - jnp.mean(values, axis=-1, keepdims=True)).astype(jnp.bfloat16)
    for block in range(base_ref.shape[0] // columns):
        place = by_device(block) * columns
        out_ref[place : place + columns] = centred[block * columns : (block + 1) * columns]


def pack_kernel(*refs):
    packed_ref = refs[-1]
    channels = packed_ref.shape[1]
    packed_ref[...] = jnp.zeros_like(packed_ref)
    places = (GAIN, SHIFT, ROW_GATE, ROW_EXIT, COL_GATE, COL_EXIT, SECOND, FIRST)
    for place, ref in zip(places, refs):
        count, width = ref.shape
        for j in range(count):
            for k in range(width // channels):
                row = place + j + k
                packed_ref[row : row + 1] = ref[j : j + 1, k * channels : (k + 1) * channels]


def spans(rows, block):
    return [slice(start, min(start + block, rows)) for start in range(0, rows, block)]


def project(residual_ref, entry_ref, gain, shift, gate, query_ref, key_ref, value_ref, gate_ref):
    rows, channels = residual_ref.shape
    scale = LOG2E * (channels // HEADS) ** -0.5
    for span in spans(rows, PROJECT_ROWS):
        normed = normalize(residual_ref[span, :].astype(jnp.float32), gain, shift)
        query_ref[span, :] = (matmul(normed, entry_ref[:, :channels]) * scale).astype(jnp.bfloat16)
        key_ref[span, :] = matmul(normed, entry_ref[:, channels : 2 * channels]).astype(jnp.bfloat16)
        value = matmul(normed, entry_ref[:, 2 * channels : 3 * channels]).astype(jnp.bfloat16)
        for tile in range(channels // LANES):
            value_ref[tile, span, :LANES] = value[:, tile * LANES : (tile + 1) * LANES]
            value_ref[tile, span, LANES:] = jnp.ones((normed.shape[0], LANES), jnp.bfloat16)
        gate_ref[span, :] = jax.nn.sigmoid(matmul(normed, entry_ref[:, 3 * channels :]) + gate)


def attend(queries, gates, key_ref, value_ref, early=False):
    channels = queries.shape[1]
    head_size = channels // HEADS
    per_tile = LANES // head_size
    lane_head = lax.broadcasted_iota(jnp.int32, (1, LANES), 1) // head_size

    def score(number):
        tile, head = divmod(number, per_tile)
        lanes = slice(tile * LANES, (tile + 1) * LANES)
        mask = (lane_head == head).astype(jnp.float32)
        return lax.dot_general(
            queries[:, lanes] * mask.astype(jnp.bfloat16),
            key_ref[:, lanes],
            (((1,), (1,)), ((), ())),
            preferred_element_type=jnp.float32,
        )

    gated = []
    following = score(0) if early else None
    for number in range(HEADS):
        scores = following if early else score(number)
        if early and number + 1 < HEADS:
            following = score(number + 1)
        tile, head = divmod(number, per_tile)
        peak = jnp.max(scores, axis=-1, keepdims=True)
        weights = jnp.exp2(scores - peak).astype(jnp.bfloat16)
        result = matmul(weights, value_ref[tile])
        ratio = result[:, :LANES] / result[:, LANES:]
        mixed = ratio if head == 0 else jnp.where(lane_head == head, ratio, mixed)
        if head + 1 == per_tile:
            gates_here = gates[:, tile * LANES : (tile + 1) * LANES]
            gated.append((gates_here * mixed).astype(jnp.bfloat16))
    return jnp.concatenate(gated, axis=1)


def for_core(ref, columns, core):
    size = Z_HIGH * columns
    return jnp.concatenate(
        [
            ref[pl.ds(pl.multiple_of(first + core * size, columns), size), :]
            for first in range(0, ref.shape[0], CORES * size)
        ],
        axis=0,
    )


def after_row(columns, core, residual_ref, exit_ref, packed_ref, query_ref, key_ref, value_ref, gate_ref):
    gated = attend(
        for_core(query_ref, columns, core), for_core(gate_ref, columns, core), key_ref, value_ref
    )
    update = matmul(gated, exit_ref[...]) + packed_ref[ROW_EXIT : ROW_EXIT + 1]
    return (for_core(residual_ref, columns, core).astype(jnp.float32) + update).astype(jnp.bfloat16)


def row_send_kernel(columns, core_ref, residual_ref, entry_ref, exit_ref, packed_ref, out_ref, *work):
    project(
        residual_ref,
        entry_ref,
        packed_ref[GAIN : GAIN + 1],
        packed_ref[SHIFT : SHIFT + 1],
        packed_ref[ROW_GATE : ROW_GATE + 1],
        *work,
    )
    out_ref[...] = after_row(columns, 1 - core_ref[0], residual_ref, exit_ref, packed_ref, *work)


def row_keep_kernel(columns, core_ref, residual_ref, exit_ref, packed_ref, *refs):
    *work, out_ref = refs
    out_ref[...] = after_row(columns, core_ref[0], residual_ref, exit_ref, packed_ref, *work)


def turn_kernel(columns, core_ref, kept_ref, received_ref, *refs):
    out_ref, turned_ref = refs[-2:]
    half = kept_ref.shape[0]
    chips = half // columns
    own = jnp.full((1, LANES), core_ref[0], jnp.int32) == 0
    for tile in range(turned_ref.shape[0]):
        lanes = slice(tile * LANES, (tile + 1) * LANES)
        kept = kept_ref[:, lanes].astype(jnp.float32)
        received = received_ref[:, lanes].astype(jnp.float32)
        for core, values in enumerate(
            (jnp.where(own, kept, received), jnp.where(own, received, kept))
        ):
            for chip in range(chips):
                turned_ref.at[tile][pl.ds(chip * CORES + core, columns, stride=CORES * chips), :] = (
                    values[chip * columns : (chip + 1) * columns]
                )
        out_ref[:, lanes] = turned_ref[tile].astype(jnp.bfloat16)


def col_kernel(residual_ref, entry_ref, exit_ref, first_ref, second_ref, packed_ref, out_ref, *work):
    rows, channels = residual_ref.shape
    project(
        residual_ref,
        entry_ref,
        packed_ref[GAIN + 1 : GAIN + 2],
        packed_ref[SHIFT + 1 : SHIFT + 2],
        packed_ref[COL_GATE : COL_GATE + 1],
        *work,
    )
    query_ref, key_ref, value_ref, gate_ref = work
    for span in spans(rows, QUERY_ROWS):
        after = residual_ref[span, :].astype(jnp.float32) + (
            matmul(
                attend(query_ref[span, :], gate_ref[span, :], key_ref, value_ref, True), exit_ref[...]
            ) + packed_ref[COL_EXIT : COL_EXIT + 1]
        )
        normed = normalize(after, packed_ref[GAIN + 2 : GAIN + 3], packed_ref[SHIFT + 2 : SHIFT + 3])
        update = packed_ref[SECOND : SECOND + 1]
        for part in range(first_ref.shape[1] // channels):
            hidden = slice(part * channels, (part + 1) * channels)
            inner = jnp.maximum(
                matmul(normed, first_ref[:, hidden]) + packed_ref[FIRST + part : FIRST + part + 1], 0.0
            )
            update = update + matmul(inner.astype(jnp.bfloat16), second_ref[hidden, :])
        out_ref[span, :] = (after + update).astype(jnp.bfloat16)


def home_kernel(residues, base_ref, values_ref, out_hbm, turned_ref, out_ref, sem):
    rows = base_ref.shape[0]
    seqs = rows // residues
    for tile in range(turned_ref.shape[0]):
        lanes = slice(tile * LANES, (tile + 1) * LANES)
        for item in range(residues):
            turned_ref.at[tile][pl.ds(item, seqs, stride=residues), :] = values_ref[
                item * seqs : (item + 1) * seqs, lanes
            ].astype(jnp.float32)
    parts = sem.shape[0]
    part = rows // parts
    copies = []
    for i in range(parts):
        span = slice(i * part, (i + 1) * part)
        mean = jnp.mean(base_ref[span, :], axis=-1, keepdims=True)
        for tile in range(turned_ref.shape[0]):
            lanes = slice(tile * LANES, (tile + 1) * LANES)
            out_ref[span, lanes] = turned_ref[tile, span, :] + mean
        copy = pltpu.make_async_copy(
            out_ref.at[pl.ds(i * part, part)], out_hbm.at[pl.ds(i * part, part)], sem.at[i]
        )
        copy.start()
        copies.append(copy)
    for copy in copies:
        copy.wait()


def call(kernel, out_shape, scratch=(), flops=0, transcendentals=0, name=None, **specs):
    return pl.pallas_call(
        kernel,
        out_shape=out_shape,
        scratch_shapes=list(scratch),
        compiler_params=pltpu.CompilerParams(vmem_limit_bytes=VMEM_LIMIT),
        cost_estimate=pl.CostEstimate(
            flops=flops, bytes_accessed=2**21, transcendentals=transcendentals
        ),
        name=name,
        **specs,
    )


def exchange(values, axes):
    count = lax.axis_size(axes)
    rows, channels = values.shape
    return lax.all_to_all(
        values.reshape(count, rows // count, channels), axes, split_axis=0, concat_axis=0, tiled=True
    ).reshape(rows, channels)


def shards(
    alignment_tensor,
    standardizer_factors,
    standardizer_offsets,
    horizontal_entry_matrix,
    horizontal_sigmoid_offset,
    horizontal_exit_matrix,
    horizontal_exit_offset,
    vertical_entry_matrix,
    vertical_sigmoid_offset,
    vertical_exit_matrix,
    vertical_exit_offset,
    feedforward_first_matrix,
    feedforward_first_offset,
    feedforward_second_matrix,
    feedforward_second_offset,
):
    seq_local, res_local, channels = alignment_tensor.shape
    rows = seq_local * res_local
    seq_count = lax.axis_size(SEQ)
    base = alignment_tensor.reshape(rows, channels)
    narrow = jax.ShapeDtypeStruct((rows, channels), jnp.bfloat16)
    wide = jax.ShapeDtypeStruct((rows, channels), jnp.float32)
    split = pltpu.VMEM((channels // LANES, rows, LANES), jnp.float32)
    work = [
        pltpu.VMEM((rows, channels), jnp.bfloat16),
        pltpu.VMEM((rows, channels), jnp.bfloat16),
        pltpu.VMEM((channels // LANES, rows, 2 * LANES), jnp.bfloat16),
        pltpu.VMEM((rows, channels), jnp.float32),
    ]
    exps = HEADS * rows * rows
    attention_flops = 10 * rows * channels * channels + 4 * rows * rows * channels
    small = [
        standardizer_factors,
        standardizer_offsets,
        horizontal_sigmoid_offset.reshape(1, -1),
        horizontal_exit_offset.reshape(1, -1),
        vertical_sigmoid_offset.reshape(1, -1),
        vertical_exit_offset.reshape(1, -1),
        feedforward_second_offset.reshape(1, -1),
        feedforward_first_offset.reshape(1, -1),
    ]
    vmem = pl.BlockSpec(memory_space=pltpu.VMEM)
    packed = call(
        pack_kernel, jax.ShapeDtypeStruct((PACKED, channels), jnp.float32), name="pack"
    )(*small, horizontal_entry_matrix, horizontal_exit_matrix)
    centred = call(functools.partial(centre_kernel, seq_count), narrow, name="centre")(base)
    core = lax.axis_index("core").astype(jnp.int32).reshape(1)
    smem = pl.BlockSpec(memory_space=pltpu.SMEM)
    half = jax.ShapeDtypeStruct((rows // CORES, channels), jnp.bfloat16)
    residual = exchange(centred, ("y", "core", "z_high"))
    sent, *projected = call(
        functools.partial(row_send_kernel, seq_count),
        (half, *(jax.ShapeDtypeStruct(array.shape, array.dtype) for array in work)),
        flops=attention_flops // 2,
        transcendentals=exps // 2,
        name="row_attention_send",
        in_specs=[smem] + [vmem] * 4,
        out_specs=(vmem,) * 5,
    )(core, residual, horizontal_entry_matrix, horizontal_exit_matrix, packed)
    received = lax.ppermute(sent, "core", [(i, CORES - 1 - i) for i in range(CORES)])
    kept = call(
        functools.partial(row_keep_kernel, seq_count),
        half,
        flops=attention_flops // 2,
        transcendentals=exps // 2,
        name="row_attention_keep",
        in_specs=[smem] + [vmem] * 7,
        out_specs=vmem,
    )(core, residual, horizontal_exit_matrix, packed, *projected)
    col_weights = (
        vertical_entry_matrix,
        vertical_exit_matrix,
        feedforward_first_matrix,
        feedforward_second_matrix,
    )
    by_chip = call(
        functools.partial(turn_kernel, seq_count),
        narrow,
        [split],
        name="turn",
        in_specs=[smem] + [vmem] * 6,
        out_specs=vmem,
    )(core, kept, received, *col_weights)
    updated = call(
        col_kernel,
        narrow,
        work,
        flops=attention_flops + 16 * rows * channels * channels,
        transcendentals=exps,
        name="col_attention_transition",
    )(
        exchange(by_chip, SEQ + ("y", "z_high")),
        *col_weights,
        packed,
    )
    home = call(
        functools.partial(home_kernel, res_local),
        wide,
        [split, pltpu.VMEM((rows, channels), jnp.float32), pltpu.SemaphoreType.DMA((3,))],
        name="home",
        in_specs=[vmem, vmem],
        out_specs=pl.BlockSpec(memory_space=pl.ANY),
    )(base, exchange(updated, SEQ))
    return home.reshape(seq_local, res_local, channels)


def solution(mesh):
    axes = ("z_low", "x", "z_high", "y", "core")
    cut = Mesh(mesh.devices.reshape(Z_LOW, X, Z_HIGH, -1, CORES), axes)
    placed = P(axes[:2], axes[2:], None)
    return jax.shard_map(
        shards, mesh=cut, in_specs=(placed,) + (P(),) * 14, out_specs=placed, check_vma=False
    )
```
